32 devices in a mesh: groups: 2 (over x), replica: 8 (over z, y), tensor: 2 (over core).
Axes of the slice: x: 2, y: 2, z: 4, core: 2. Of those that a mesh axis runs over, the one named last changes fastest.
Arguments:
- tokens: bfloat16 [4096, 8192], P(('groups', 'replica'), 'tensor'), parts along dimension 0, may hold values from -6 to 6
- value_weight: bfloat16 [8192, 1024], P('tensor'), may hold values from -0.0625 to 0.0625
- adapter_down: bfloat16 [256, 8192, 64], P(None, ('tensor', 'replica')), may hold values from -0.0625 to 0.0625
- adapter_up: bfloat16 [256, 64, 1024], P(None, None, 'replica'), may hold values from -0.75 to 0.75
- adapter_per_block: int32 [32], P(('groups', 'replica')), parts along dimension 0, may hold values from 0 to 255
- block_live: int32 [32], P(('groups', 'replica')), parts along dimension 0, may hold values from 1 to 128
Outputs:
- values_out: bfloat16 [4096, 1024], P(('groups', 'replica'), 'tensor'), parts along dimension 0
The draws below stay inside these ranges and needn't reach their ends.
There are 2 independent parts, one for each index of `groups`. The reference program is written for one: setup_inputs(seed, part) draws one part's arguments, and reference() takes and returns one part's arrays. A program takes and returns all parts, laid end to end along the dimension named above; an argument that names none is the same for every part. Nothing has to cross between parts.
All inputs are finite; a program needn't handle non-finite values.
Results may differ from the reference program's by a relative error of at most 0.0039.
Values may be sent and summed in bfloat16 or wider, within the bound.
A program may use at most 128 MiB of HBM per device.

```python
import math
import jax
import jax.numpy as jnp
import numpy as np
from jax import lax

D = 8192
VALUE_OUT_WIDTH = 1024
RANK = 64
BLOCK = 128
ADAPTERS = 256
TOKEN_SLOTS = 2048
NBLK = 16


def touch_ends(result, own_key, smallest, high):
    extent = result.shape
    place = [jax.random.randint(jax.random.fold_in(own_key, axis), (), 0, extent[axis]) for axis in range(len(extent))]
    result = result.at[tuple(place)].set(smallest)
    longest = extent.index(max(extent))
    place[longest] = (place[longest] + 1) % extent[longest]
    return result.at[tuple(place)].set(high)


def levels(stream_key, extent, shards, smallest, high):
    loudness = 1.0
    for axis_at, shards_of in shards:
        steps = jax.random.uniform(jax.random.fold_in(jax.random.fold_in(stream_key, 6), axis_at), (shards_of,), jnp.float32, smallest / len(shards), high / len(shards))
        loudness = loudness * jnp.repeat(jnp.exp(steps), extent[axis_at] // shards_of).reshape((-1,) + (1,) * (len(extent) - 1 - axis_at))
    return loudness


def cumulative_ranks(number_of, skew):
    weights = [(1 << 20) // math.isqrt(standing ** skew) + 1 for standing in range(1, number_of + 1)]
    deviation = 1 + sum(weights) // (1 << 30)
    return np.cumsum(np.array([max(1, weight // deviation) for weight in weights]))


def ranked(rng, extent, number_of, lean):
    table = cumulative_ranks(number_of, lean)
    pick = jax.random.randint(jax.random.fold_in(rng, 1), extent, 0, int(table[number_of - 1]))
    grade = jnp.searchsorted(jnp.asarray(table, jnp.int32), pick, side="right")
    return jax.random.permutation(jax.random.fold_in(rng, 2), number_of)[grade].astype(jnp.int32)


def normal_values(stream_key, shape, scale, bound, split=(), kind=jnp.bfloat16):
    drawn = scale * jax.random.normal(stream_key, shape, jnp.float32)
    if split:
        drawn = drawn * levels(stream_key, shape, split, -0.22, 0.18)
    return jnp.clip(drawn, -bound, bound).astype(kind)


def setup_inputs(seed: int = 0, part: int = 0) -> dict:
    splits = jax.random.split(jax.random.key(seed), 7)
    own_keys = jax.random.split(jax.random.fold_in(splits[6], part), 7)
    tokens = normal_values(own_keys[0], (TOKEN_SLOTS, D), 1.0, 6.0, ((0, 8), (1, 2)))
    value_weight = normal_values(splits[1], (D, VALUE_OUT_WIDTH), D ** -0.5, 0.0625, ((0, 2),))
    adapter_down = normal_values(splits[2], (ADAPTERS, D, RANK), D ** -0.5, 0.0625, ((1, 16),))
    adapter_up = normal_values(splits[3], (ADAPTERS, RANK, VALUE_OUT_WIDTH), RANK ** -0.5, 0.75, ((2, 8),))
    adapter_per_block = touch_ends(ranked(own_keys[4], (NBLK,), ADAPTERS, 2), jax.random.fold_in(own_keys[4], 3), 0, ADAPTERS - 1).astype(jnp.int32)
    block_live = touch_ends(jax.random.randint(own_keys[5], (NBLK,), 1, BLOCK + 1), jax.random.fold_in(own_keys[5], 1), 1, BLOCK).astype(jnp.int32)
    return dict(tokens=tokens, value_weight=value_weight, adapter_down=adapter_down, adapter_up=adapter_up, adapter_per_block=adapter_per_block, block_live=block_live)


def reference(tokens, value_weight, adapter_down, adapter_up, adapter_per_block, block_live):
    base_value_sum = jnp.dot(tokens, value_weight, preferred_element_type=jnp.float32)
    token_blocks = tokens.reshape(NBLK, BLOCK, D)

    def tokens_per_block(operands):
        row_block, adapter_id = operands
        down = lax.dynamic_index_in_dim(adapter_down, adapter_id, 0, keepdims=False)
        up = lax.dynamic_index_in_dim(adapter_up, adapter_id, 0, keepdims=False)
        shrink = jnp.dot(row_block, down, preferred_element_type=jnp.float32)
        shrunk = shrink.astype(jnp.bfloat16)
        return jnp.dot(shrunk, up, preferred_element_type=jnp.float32)

    adapter_delta = lax.map(tokens_per_block, (token_blocks, adapter_per_block)).reshape(TOKEN_SLOTS, VALUE_OUT_WIDTH)
    position = jnp.arange(BLOCK, dtype=jnp.int32)
    active_mask = (position[None, :] < block_live[:, None]).reshape(TOKEN_SLOTS, 1)
    combined_output = jnp.where(active_mask, base_value_sum + adapter_delta, 0.0)
    return combined_output.astype(jnp.bfloat16)
```

```python
import jax
import jax.numpy as jnp
from jax import lax
from jax.sharding import PartitionSpec as P

BLOCK = 128


def local(tokens, value_weight, adapter_down, adapter_up, adapter_per_block, block_live):
    replicas = lax.axis_size("replica")
    cores = lax.axis_size("tensor")
    core = lax.axis_index("tensor")
    rows, features = tokens.shape
    blocks = rows // BLOCK
    part, rank = adapter_down.shape[1:]
    out_width = value_weight.shape[1]
    half = out_width // cores
    every_id = lax.all_gather(adapter_per_block, "replica", axis=0, tiled=True)
    down = jnp.swapaxes(adapter_down, 1, 2)[every_id]
    down = down.reshape(replicas, blocks, rank, part)
    down = lax.all_to_all(down, "replica", split_axis=0, concat_axis=0, tiled=True)
    up = adapter_up[every_id].reshape(replicas, blocks, rank, -1)
    up = lax.all_to_all(up, "replica", split_axis=0, concat_axis=0, tiled=True)
    owners = replicas // cores
    up = lax.dynamic_slice_in_dim(up, core * owners, owners, 0)
    base = jnp.dot(tokens, value_weight, preferred_element_type=jnp.float32)
    base = lax.psum_scatter(base, "tensor", scatter_dimension=1, tiled=True)
    blocked = tokens.reshape(blocks, BLOCK, replicas, part)
    shrink = jnp.einsum("bksf,sbrf->bkr", blocked, down, preferred_element_type=jnp.float32)
    shrunk = lax.psum(shrink, "tensor").astype(jnp.bfloat16)
    delta = jnp.einsum("bkr,sbrc->bksc", shrunk, up, preferred_element_type=jnp.float32)
    combined = base + delta.reshape(rows, half)
    position = jnp.arange(BLOCK, dtype=jnp.int32)
    live = (position[None, :] < block_live[:, None]).reshape(rows, 1)
    return jnp.where(live, combined, 0.0).astype(jnp.bfloat16)


def solution(mesh):
    return jax.shard_map(
        local,
        mesh=mesh,
        in_specs=(
            P(("groups", "replica"), "tensor"),
            P("tensor", None),
            P(None, ("tensor", "replica"), None),
            P(None, None, "replica"),
            P(("groups", "replica")),
            P(("groups", "replica")),
        ),
        out_specs=P(("groups", "replica"), "tensor"),
        check_vma=False,
    )
```

```python
import functools

import jax
import jax.numpy as jnp
from jax import lax
from jax.experimental import pallas as pl
from jax.experimental.pallas import tpu as pltpu
from jax.sharding import PartitionSpec as P

BLOCK = 128
LANES = 128
TABLE_PIECES = 8
MESH = pl.DeviceIdType.MESH


def nearest_last(replicas):
    middle = replicas // 2
    return sorted(range(1, replicas), key=lambda k: (abs(k - middle), k))


def fused_kernel(
    replicas,
    ids_ref,
    tokens_hbm,
    weight_hbm,
    down_hbm,
    up_hbm,
    out_ref,
    all_ids,
    down_table,
    up_table,
    tokens,
    weight,
    down_out,
    up_out,
    down_in,
    up_in,
    base,
    base_out,
    base_in,
    shrink_out,
    shrink_in,
    table_sem,
    local_sem,
    id_send,
    id_recv,
    down_send,
    down_recv,
    up_send,
    up_recv,
    pair_send,
    pair_recv,
):
    me = lax.axis_index("replica")
    core = lax.axis_index("tensor")
    sibling = 1 - core
    blocks = ids_ref.shape[0]
    rank, part = down_table.shape[1:]
    rows = tokens.shape[0]
    half = out_ref.shape[1]
    columns = up_table.shape[2]
    owners = half // columns
    offsets = nearest_last(replicas)
    owner_core = me // owners

    step = down_table.shape[0] // TABLE_PIECES
    table_copies = [
        pltpu.make_async_copy(
            down_hbm.at[pl.ds(i * step, step)], down_table.at[pl.ds(i * step, step)], table_sem.at[i]
        )
        for i in range(TABLE_PIECES)
    ]
    for copy in table_copies:
        copy.start()
    up_copy = pltpu.make_async_copy(up_hbm, up_table, local_sem.at[0])
    up_copy.start()
    tokens_copy = pltpu.make_async_copy(tokens_hbm, tokens, local_sem.at[1])
    weight_copies = [
        pltpu.make_async_copy(
            weight_hbm.at[:, pl.ds(c * half, half)], weight.at[:, pl.ds(c * half, half)], local_sem.at[2 + c]
        )
        for c in range(2)
    ]

    barrier = pltpu.get_barrier_semaphore()
    for k in offsets:
        pl.semaphore_signal(
            barrier, inc=1, device_id={"replica": lax.rem(me + k, replicas)}, device_id_type=MESH
        )
    pl.semaphore_signal(barrier, inc=1, device_id={"tensor": sibling}, device_id_type=MESH)
    pl.semaphore_wait(barrier, replicas)

    id_copies = []
    for k in offsets:
        copy = pltpu.make_async_remote_copy(
            src_ref=ids_ref,
            dst_ref=all_ids.at[k],
            send_sem=id_send.at[k],
            recv_sem=id_recv.at[k],
            device_id={"replica": lax.rem(me + k, replicas)},
            device_id_type=MESH,
        )
        copy.start()
        id_copies.append(copy)
    for copy in table_copies:
        copy.wait()
    up_copy.wait()
    tokens_copy.start()
    for copy in weight_copies:
        copy.start()
    for copy in id_copies:
        copy.wait()

    down_copies, up_copies = {}, {}
    for k in offsets:
        peer = {"replica": lax.rem(me + k, replicas)}
        for j in range(blocks):
            down_out[k, j] = down_table[all_ids[replicas - k, j]]
        down_copies[k] = pltpu.make_async_remote_copy(
            src_ref=down_out.at[k],
            dst_ref=down_in.at[k],
            send_sem=down_send.at[k],
            recv_sem=down_recv.at[k],
            device_id=peer,
            device_id_type=MESH,
        )
        down_copies[k].start()
        up_copies[k] = pltpu.make_async_remote_copy(
            src_ref=up_out.at[k],
            dst_ref=up_in.at[lax.rem(me, owners)],
            send_sem=up_send.at[k],
            recv_sem=up_recv.at[lax.rem(me, owners)],
            device_id=peer,
            device_id_type=MESH,
        )

        @pl.when(owner_core == core)
        def _():
            for j in range(blocks):
                up_out[k, j] = up_table[all_ids[replicas - k, j]]
            up_copies[k].start()

    for j in range(blocks):
        down_in[0, j] = down_table[ids_ref[j]]

    @pl.when(owner_core == core)
    def _():
        for j in range(blocks):
            up_in[lax.rem(me, owners), j] = up_table[ids_ref[j]]

    tokens_copy.wait()
    for copy in weight_copies:
        copy.wait()
    tile = 256

    def base_tile(column):
        return jnp.dot(
            tokens[...],
            weight[:, pl.ds(pl.multiple_of(column, tile), tile)],
            preferred_element_type=jnp.float32,
        )

    @pl.loop(0, half // tile)
    def _(i):
        base_out[:, pl.ds(pl.multiple_of(i * tile, tile), tile)] = base_tile(sibling * half + i * tile)

    base_copy = pltpu.make_async_remote_copy(
        src_ref=base_out,
        dst_ref=base_in,
        send_sem=pair_send.at[0],
        recv_sem=pair_recv.at[0],
        device_id={"tensor": sibling},
        device_id_type=MESH,
    )
    base_copy.start()

    @pl.loop(0, half // tile)
    def _(i):
        base[:, pl.ds(pl.multiple_of(i * tile, tile), tile)] = base_tile(core * half + i * tile)

    def add_part(k, first):
        column = pl.multiple_of(lax.rem(me + replicas - k, replicas) * part, LANES)
        for j in range(blocks):
            span = pl.ds(j * BLOCK, BLOCK)
            term = lax.dot_general(
                tokens[span, pl.ds(column, part)],
                down_in[k, j],
                (((1,), (1,)), ((), ())),
                preferred_element_type=jnp.float32,
            )
            shrink_out[span, :] = term if first else shrink_out[span, :] + term

    add_part(0, True)
    base_copy.wait()
    base[...] += base_in[...]
    for k in reversed(offsets):
        down_copies[k].wait_recv()
        add_part(k, False)

    shrink_copy = pltpu.make_async_remote_copy(
        src_ref=shrink_out,
        dst_ref=shrink_in,
        send_sem=pair_send.at[1],
        recv_sem=pair_recv.at[1],
        device_id={"tensor": sibling},
        device_id_type=MESH,
    )
    shrink_copy.start()
    for s in range(owners):
        arriving = pltpu.make_async_remote_copy(
            src_ref=up_out.at[0],
            dst_ref=up_in.at[s],
            send_sem=up_send.at[0],
            recv_sem=up_recv.at[s],
            device_id={"replica": lax.rem(me + 1, replicas)},
            device_id_type=MESH,
        )

        @pl.when(core * owners + s != me)
        def _():
            arriving.wait_recv()

    shrink_copy.wait()
    shrunk = (shrink_out[...] + shrink_in[...]).astype(jnp.bfloat16)
    for s in range(owners):
        for j in range(blocks):
            span = pl.ds(j * BLOCK, BLOCK)
            delta = jnp.dot(
                shrunk[j * BLOCK : (j + 1) * BLOCK], up_in[s, j], preferred_element_type=jnp.float32
            )
            wide = pl.ds(s * columns, columns)
            out_ref[span, wide] = (base[span, wide] + delta).astype(out_ref.dtype)

    for k in offsets:
        down_copies[k].wait_send()

    @pl.when(owner_core == core)
    def _():
        for k in offsets:
            up_copies[k].wait_send()


def fused(replicas, tokens, value_weight, adapter_down, adapter_up, adapter_per_block):
    rows, features = tokens.shape
    adapters, part, rank = adapter_down.shape
    blocks = rows // BLOCK
    out_width = value_weight.shape[1]
    half = out_width // 2
    columns = adapter_up.shape[2]
    owners = half // columns
    dma = pltpu.SemaphoreType.DMA
    return pl.pallas_call(
        functools.partial(fused_kernel, replicas),
        out_shape=jax.ShapeDtypeStruct((rows, half), jnp.bfloat16),
        in_specs=[pl.BlockSpec(memory_space=pltpu.SMEM)] + [pl.BlockSpec(memory_space=pl.ANY)] * 4,
        out_specs=pl.BlockSpec(memory_space=pltpu.VMEM),
        scratch_shapes=[
            pltpu.SMEM((replicas, blocks), jnp.int32),
            pltpu.VMEM((adapters, rank, part), jnp.bfloat16),
            pltpu.VMEM((adapters, rank, columns), jnp.bfloat16),
            pltpu.VMEM((rows, features), jnp.bfloat16),
            pltpu.VMEM((features, out_width), jnp.bfloat16),
            pltpu.VMEM((replicas, blocks, rank, part), jnp.bfloat16),
            pltpu.VMEM((replicas, blocks, rank, columns), jnp.bfloat16),
            pltpu.VMEM((replicas, blocks, rank, part), jnp.bfloat16),
            pltpu.VMEM((owners, blocks, rank, columns), jnp.bfloat16),
            pltpu.VMEM((rows, half), jnp.float32),
            pltpu.VMEM((rows, half), jnp.float32),
            pltpu.VMEM((rows, half), jnp.float32),
            pltpu.VMEM((rows, rank), jnp.float32),
            pltpu.VMEM((rows, rank), jnp.float32),
            dma((TABLE_PIECES,)),
            dma((4,)),
            dma((replicas,)),
            dma((replicas,)),
            dma((replicas,)),
            dma((replicas,)),
            dma((replicas,)),
            dma((owners,)),
            dma((2,)),
            dma((2,)),
        ],
        compiler_params=pltpu.CompilerParams(
            collective_id=0, has_side_effects=True, vmem_limit_bytes=56 * 1024 * 1024
        ),
        cost_estimate=pl.CostEstimate(
            flops=2 * rows * features * (out_width + rank), bytes_accessed=32 * 1024 * 1024, transcendentals=0
        ),
    )(adapter_per_block, tokens, value_weight, jnp.swapaxes(adapter_down, 1, 2), adapter_up)


def spread(replicas, tokens, value_weight, adapter_down, adapter_up, adapter_per_block):
    cores = lax.axis_size("tensor")
    core = lax.axis_index("tensor")
    rows = tokens.shape[0]
    blocks = rows // BLOCK
    part, rank = adapter_down.shape[1:]
    half = value_weight.shape[1] // cores
    every_id = lax.all_gather(adapter_per_block, "replica", axis=0, tiled=True)
    down = jnp.swapaxes(adapter_down, 1, 2)[every_id]
    down = down.reshape(replicas, blocks, rank, part)
    down = lax.all_to_all(down, "replica", split_axis=0, concat_axis=0, tiled=True)
    up = adapter_up[every_id].reshape(replicas, blocks, rank, -1)
    up = lax.all_to_all(up, "replica", split_axis=0, concat_axis=0, tiled=True)
    owners = replicas // cores
    up = lax.dynamic_slice_in_dim(up, core * owners, owners, 0)
    base = jnp.dot(tokens, value_weight, preferred_element_type=jnp.float32)
    base = lax.psum_scatter(base, "tensor", scatter_dimension=1, tiled=True)
    blocked = tokens.reshape(blocks, BLOCK, replicas, part)
    shrink = jnp.einsum("bksf,sbrf->bkr", blocked, down, preferred_element_type=jnp.float32)
    shrunk = lax.psum(shrink, "tensor").astype(jnp.bfloat16)
    delta = jnp.einsum("bkr,sbrc->bksc", shrunk, up, preferred_element_type=jnp.float32)
    return base + delta.reshape(rows, half)


def local(tokens, value_weight, adapter_down, adapter_up, adapter_per_block, block_live):
    replicas = lax.axis_size("replica")
    cores = lax.axis_size("tensor")
    half = value_weight.shape[1] // cores
    part, columns = adapter_down.shape[1], adapter_up.shape[2]
    aligned = part % LANES == 0 and columns % LANES == 0 and half % 256 == 0
    inner = fused if aligned and cores == 2 and half % columns == 0 else spread
    combined = inner(replicas, tokens, value_weight, adapter_down, adapter_up, adapter_per_block)
    position = jnp.arange(BLOCK, dtype=jnp.int32)
    live = (position[None, :] < block_live[:, None]).reshape(tokens.shape[0], 1)
    return jnp.where(live, combined, 0).astype(jnp.bfloat16)


def solution(mesh):
    return jax.shard_map(
        local,
        mesh=mesh,
        in_specs=(
            P(("groups", "replica"), "tensor"),
            P("tensor", None),
            P(None, ("tensor", "replica"), None),
            P(None, None, "replica"),
            P(("groups", "replica")),
            P(("groups", "replica")),
        ),
        out_specs=P(("groups", "replica"), "tensor"),
        check_vma=False,
    )
```

```python
import functools

import jax
import jax.numpy as jnp
from jax import lax
from jax.experimental import pallas as pl
from jax.experimental.pallas import tpu as pltpu
from jax.sharding import PartitionSpec as P

BLOCK = 128
LANES = 128
CUTS = ((0, 1), (1, 3))
MESH = pl.DeviceIdType.MESH


def partners(replicas, me):
    middle = replicas // 2
    order = [*range(middle - 1, middle + 2), *range(middle - 2, 0, -1), *range(middle + 2, replicas)]
    return [(k, lax.rem(me + k, replicas), lax.rem(me + replicas - k, replicas)) for k in order]


def fused_kernel(
    replicas,
    ids_ref,
    live_ref,
    tokens_hbm,
    weight_hbm,
    down_hbm,
    up_hbm,
    out_ref,
    all_ids,
    head_table,
    tail_table,
    up_table,
    tokens,
    weight,
    down_out,
    up_out,
    down_in,
    up_in,
    base,
    base_out,
    base_in,
    shrink_out,
    shrink_in,
    table_sem,
    local_sem,
    id_send,
    id_recv,
    down_send,
    down_recv,
    up_send,
    up_recv,
    pair_send,
    pair_recv,
):
    me = lax.axis_index("replica")
    core = lax.axis_index("tensor")
    sibling = 1 - core
    blocks = ids_ref.shape[0]
    rank, part = down_in.shape[2:]
    rows = tokens.shape[0]
    half = out_ref.shape[1]
    columns = up_table.shape[2]
    owners = half // columns
    peers = partners(replicas, me)
    owner_core = me // owners

    cuts = [(cut * rank // 4, size * rank // 4) for cut, size in CUTS]
    tables = [head_table, tail_table]
    table_copies = [
        pltpu.make_async_copy(
            down_hbm.at[:, pl.ds(cut, size)], tables[i], table_sem.at[i]
        )
        for i, (cut, size) in enumerate(cuts)
    ]
    for copy in table_copies:
        copy.start()
    up_copy = pltpu.make_async_copy(up_hbm, up_table, local_sem.at[0])
    tokens_copy = pltpu.make_async_copy(tokens_hbm, tokens, local_sem.at[1])
    weight_copies = [
        pltpu.make_async_copy(
            weight_hbm.at[:, pl.ds(c * half, half)], weight.at[:, pl.ds(c * half, half)], local_sem.at[2 + c]
        )
        for c in range(2)
    ]

    barrier = pltpu.get_barrier_semaphore()
    for _, to, _ in peers:
        pl.semaphore_signal(barrier, inc=1, device_id={"replica": to}, device_id_type=MESH)
    pl.semaphore_signal(barrier, inc=1, device_id={"tensor": sibling}, device_id_type=MESH)
    pl.semaphore_wait(barrier, replicas)

    id_copies = []
    for k, to, _ in peers:
        copy = pltpu.make_async_remote_copy(
            src_ref=ids_ref,
            dst_ref=all_ids.at[k],
            send_sem=id_send.at[k],
            recv_sem=id_recv.at[k],
            device_id={"replica": to},
            device_id_type=MESH,
        )
        copy.start()
        id_copies.append(copy)
    for copy in id_copies:
        copy.wait()

    down_copies, up_copies = {}, {}
    for i, (cut, size) in enumerate(cuts):
        table_copies[i].wait()
        span = pl.ds(cut, size)
        for k, to, _ in peers:
            for j in range(blocks):
                down_out[k, j, span] = tables[i][all_ids[replicas - k, j]]
            down_copies[k, i] = pltpu.make_async_remote_copy(
                src_ref=down_out.at[k, :, span],
                dst_ref=down_in.at[k, :, span],
                send_sem=down_send.at[k, i],
                recv_sem=down_recv.at[k, i],
                device_id={"replica": to},
                device_id_type=MESH,
            )
            down_copies[k, i].start()

    @pl.when(owner_core == core)
    def _():
        up_copy.start()

    tokens_copy.start()
    for copy in weight_copies:
        copy.start()

    for j in range(blocks):
        for table, (cut, size) in zip(tables, cuts):
            down_in[0, j, pl.ds(cut, size)] = table[ids_ref[j]]

    for k, to, _ in peers:
        up_copies[k] = pltpu.make_async_remote_copy(
            src_ref=up_out.at[k],
            dst_ref=up_in.at[lax.rem(me, owners)],
            send_sem=up_send.at[k],
            recv_sem=up_recv.at[lax.rem(me, owners)],
            device_id={"replica": to},
            device_id_type=MESH,
        )

    @pl.when(owner_core == core)
    def _():
        up_copy.wait()
        for k, _, _ in peers:
            for j in range(blocks):
                up_out[k, j] = up_table[all_ids[replicas - k, j]]
            up_copies[k].start()
        for j in range(blocks):
            up_in[lax.rem(me, owners), j] = up_table[ids_ref[j]]

    tokens_copy.wait()
    for copy in weight_copies:
        copy.wait()
    tile = 256

    def base_tile(column):
        return jnp.dot(
            tokens[...],
            weight[:, pl.ds(pl.multiple_of(column, tile), tile)],
            preferred_element_type=jnp.float32,
        )

    @pl.loop(0, half // tile)
    def _(i):
        base_out[:, pl.ds(pl.multiple_of(i * tile, tile), tile)] = base_tile(sibling * half + i * tile)

    base_copy = pltpu.make_async_remote_copy(
        src_ref=base_out,
        dst_ref=base_in,
        send_sem=pair_send.at[0],
        recv_sem=pair_recv.at[0],
        device_id={"tensor": sibling},
        device_id_type=MESH,
    )
    base_copy.start()

    @pl.loop(0, half // tile)
    def _(i):
        base[:, pl.ds(pl.multiple_of(i * tile, tile), tile)] = base_tile(core * half + i * tile)

    def add_part(k, source, first):
        column = pl.multiple_of(source * part, LANES)
        for j in range(blocks):
            span = pl.ds(j * BLOCK, BLOCK)
            term = lax.dot_general(
                tokens[span, pl.ds(column, part)],
                down_in[k, j],
                (((1,), (1,)), ((), ())),
                preferred_element_type=jnp.float32,
            )
            shrink_out[span, :] = term if first else shrink_out[span, :] + term

    add_part(0, me, True)
    base_copy.wait()
    base[...] += base_in[...]
    for k, _, source in peers[::-1]:
        for i in range(len(cuts)):
            down_copies[k, i].wait_recv()
        add_part(k, source, False)

    shrink_copy = pltpu.make_async_remote_copy(
        src_ref=shrink_out,
        dst_ref=shrink_in,
        send_sem=pair_send.at[1],
        recv_sem=pair_recv.at[1],
        device_id={"tensor": sibling},
        device_id_type=MESH,
    )
    shrink_copy.start()
    for s in range(owners):
        arriving = pltpu.make_async_remote_copy(
            src_ref=up_out.at[0],
            dst_ref=up_in.at[s],
            send_sem=up_send.at[0],
            recv_sem=up_recv.at[s],
            device_id={"replica": lax.rem(me + 1, replicas)},
            device_id_type=MESH,
        )

        @pl.when(core * owners + s != me)
        def _():
            arriving.wait_recv()

    shrink_copy.wait()
    shrunk = (shrink_out[...] + shrink_in[...]).astype(jnp.bfloat16)
    for s in range(owners):
        for j in range(blocks):
            span = pl.ds(j * BLOCK, BLOCK)
            delta = jnp.dot(
                shrunk[j * BLOCK : (j + 1) * BLOCK], up_in[s, j], preferred_element_type=jnp.float32
            )
            wide = pl.ds(s * columns, columns)
            position = lax.broadcasted_iota(jnp.int32, delta.shape, 0)
            value = jnp.where(position < live_ref[j], base[span, wide] + delta, 0.0)
            out_ref[span, wide] = value.astype(out_ref.dtype)

    for copy in down_copies.values():
        copy.wait_send()

    @pl.when(owner_core == core)
    def _():
        for copy in up_copies.values():
            copy.wait_send()


def fused(replicas, tokens, value_weight, adapter_down, adapter_up, adapter_per_block, block_live):
    rows, features = tokens.shape
    adapters, part, rank = adapter_down.shape
    blocks = rows // BLOCK
    out_width = value_weight.shape[1]
    half = out_width // 2
    columns = adapter_up.shape[2]
    owners = half // columns
    dma = pltpu.SemaphoreType.DMA
    return pl.pallas_call(
        functools.partial(fused_kernel, replicas),
        out_shape=jax.ShapeDtypeStruct((rows, half), jnp.bfloat16),
        in_specs=[pl.BlockSpec(memory_space=pltpu.SMEM)] * 2 + [pl.BlockSpec(memory_space=pl.ANY)] * 4,
        out_specs=pl.BlockSpec(memory_space=pltpu.VMEM),
        scratch_shapes=[
            pltpu.SMEM((replicas, blocks), jnp.int32),
            *[pltpu.VMEM((adapters, size * rank // 4, part), jnp.bfloat16) for _, size in CUTS],
            pltpu.VMEM((adapters, rank, columns), jnp.bfloat16),
            pltpu.VMEM((rows, features), jnp.bfloat16),
            pltpu.VMEM((features, out_width), jnp.bfloat16),
            pltpu.VMEM((replicas, blocks, rank, part), jnp.bfloat16),
            pltpu.VMEM((replicas, blocks, rank, columns), jnp.bfloat16),
            pltpu.VMEM((replicas, blocks, rank, part), jnp.bfloat16),
            pltpu.VMEM((owners, blocks, rank, columns), jnp.bfloat16),
            pltpu.VMEM((rows, half), jnp.float32),
            pltpu.VMEM((rows, half), jnp.float32),
            pltpu.VMEM((rows, half), jnp.float32),
            pltpu.VMEM((rows, rank), jnp.float32),
            pltpu.VMEM((rows, rank), jnp.float32),
            dma((len(CUTS),)),
            dma((4,)),
            dma((replicas,)),
            dma((replicas,)),
            dma((replicas, len(CUTS))),
            dma((replicas, len(CUTS))),
            dma((replicas,)),
            dma((owners,)),
            dma((2,)),
            dma((2,)),
        ],
        compiler_params=pltpu.CompilerParams(
            collective_id=0, has_side_effects=True, vmem_limit_bytes=56 * 1024 * 1024
        ),
        cost_estimate=pl.CostEstimate(
            flops=2 * rows * features * (out_width + rank), bytes_accessed=32 * 1024 * 1024, transcendentals=0
        ),
    )(adapter_per_block, block_live, tokens, value_weight, jnp.swapaxes(adapter_down, 1, 2), adapter_up)


def spread(replicas, tokens, value_weight, adapter_down, adapter_up, adapter_per_block, block_live):
    cores = lax.axis_size("tensor")
    core = lax.axis_index("tensor")
    rows = tokens.shape[0]
    blocks = rows // BLOCK
    part, rank = adapter_down.shape[1:]
    half = value_weight.shape[1] // cores
    every_id = lax.all_gather(adapter_per_block, "replica", axis=0, tiled=True)
    down = jnp.swapaxes(adapter_down, 1, 2)[every_id]
    down = down.reshape(replicas, blocks, rank, part)
    down = lax.all_to_all(down, "replica", split_axis=0, concat_axis=0, tiled=True)
    up = adapter_up[every_id].reshape(replicas, blocks, rank, -1)
    up = lax.all_to_all(up, "replica", split_axis=0, concat_axis=0, tiled=True)
    owners = replicas // cores
    up = lax.dynamic_slice_in_dim(up, core * owners, owners, 0)
    base = jnp.dot(tokens, value_weight, preferred_element_type=jnp.float32)
    base = lax.psum_scatter(base, "tensor", scatter_dimension=1, tiled=True)
    blocked = tokens.reshape(blocks, BLOCK, replicas, part)
    shrink = jnp.einsum("bksf,sbrf->bkr", blocked, down, preferred_element_type=jnp.float32)
    shrunk = lax.psum(shrink, "tensor").astype(jnp.bfloat16)
    delta = jnp.einsum("bkr,sbrc->bksc", shrunk, up, preferred_element_type=jnp.float32)
    combined = base + delta.reshape(rows, half)
    position = jnp.arange(BLOCK, dtype=jnp.int32)
    live = (position[None, :] < block_live[:, None]).reshape(rows, 1)
    return jnp.where(live, combined, 0.0).astype(jnp.bfloat16)


def local(tokens, value_weight, adapter_down, adapter_up, adapter_per_block, block_live):
    replicas = lax.axis_size("replica")
    cores = lax.axis_size("tensor")
    half = value_weight.shape[1] // cores
    part, columns = adapter_down.shape[1], adapter_up.shape[2]
    aligned = part % LANES == 0 and columns % LANES == 0 and half % 256 == 0
    aligned = aligned and replicas >= 4 and adapter_down.shape[2] % 64 == 0
    inner = fused if aligned and cores == 2 and half % columns == 0 else spread
    return inner(replicas, tokens, value_weight, adapter_down, adapter_up, adapter_per_block, block_live)


def solution(mesh):
    return jax.shard_map(
        local,
        mesh=mesh,
        in_specs=(
            P(("groups", "replica"), "tensor"),
            P("tensor", None),
            P(None, ("tensor", "replica"), None),
            P(None, None, "replica"),
            P(("groups", "replica")),
            P(("groups", "replica")),
        ),
        out_specs=P(("groups", "replica"), "tensor"),
        check_vma=False,
    )
```

```python
import functools

import jax
import jax.numpy as jnp
from jax import lax
from jax.experimental import pallas as pl
from jax.experimental.pallas import tpu as pltpu
from jax.sharding import PartitionSpec as P

BLOCK = 128
LANES = 128
CUTS = ((0, 2), (2, 2))
MESH = pl.DeviceIdType.MESH


def partners(replicas, me):
    middle = replicas // 2
    order = [*range(middle - 1, middle + 2), *range(middle - 2, 0, -1), *range(middle + 2, replicas)]
    return [(k, lax.rem(me + k, replicas), lax.rem(me + replicas - k, replicas)) for k in order]


def fused_kernel(
    replicas,
    ids_ref,
    live_ref,
    tokens_hbm,
    weight_hbm,
    down_hbm,
    up_hbm,
    out_ref,
    all_ids,
    head_table,
    tail_table,
    up_table,
    tokens,
    weight,
    down_out,
    up_out,
    down_in,
    up_in,
    base,
    base_out,
    base_in,
    shrink_out,
    shrink_in,
    table_sem,
    local_sem,
    id_send,
    id_recv,
    down_send,
    down_recv,
    up_send,
    up_recv,
    pair_send,
    pair_recv,
):
    me = lax.axis_index("replica")
    core = lax.axis_index("tensor")
    sibling = 1 - core
    blocks = ids_ref.shape[0]
    rank, part = down_in.shape[2:]
    rows = tokens.shape[0]
    half = out_ref.shape[1]
    columns = up_table.shape[2]
    owners = half // columns
    peers = partners(replicas, me)
    owner_core = me // owners

    cuts = [(cut * rank // 4, size * rank // 4) for cut, size in CUTS]
    tables = [head_table, tail_table]
    table_copies = [
        pltpu.make_async_copy(
            down_hbm.at[:, pl.ds(cut, size)], tables[i], table_sem.at[i]
        )
        for i, (cut, size) in enumerate(cuts)
    ]
    for copy in table_copies:
        copy.start()
    up_copy = pltpu.make_async_copy(up_hbm, up_table, local_sem.at[0])
    tokens_copy = pltpu.make_async_copy(tokens_hbm, tokens, local_sem.at[1])
    weight_copies = [
        pltpu.make_async_copy(
            weight_hbm.at[:, pl.ds(c * half, half)], weight.at[:, pl.ds(c * half, half)], local_sem.at[2 + c]
        )
        for c in range(2)
    ]

    barrier = pltpu.get_barrier_semaphore()
    for _, to, _ in peers:
        pl.semaphore_signal(barrier, inc=1, device_id={"replica": to}, device_id_type=MESH)
    pl.semaphore_signal(barrier, inc=1, device_id={"tensor": sibling}, device_id_type=MESH)
    pl.semaphore_wait(barrier, replicas)

    id_copies = []
    for k, to, _ in peers:
        copy = pltpu.make_async_remote_copy(
            src_ref=ids_ref,
            dst_ref=all_ids.at[k],
            send_sem=id_send.at[k],
            recv_sem=id_recv.at[k],
            device_id={"replica": to},
            device_id_type=MESH,
        )
        copy.start()
        id_copies.append(copy)
    for copy in id_copies:
        copy.wait()

    down_copies, up_copies = {}, {}
    for i, (cut, size) in enumerate(cuts):
        table_copies[i].wait()
        span = pl.ds(cut, size)
        for k, to, _ in peers:
            for j in range(blocks):
                down_out[k, j, span] = tables[i][all_ids[replicas - k, j]]
            down_copies[k, i] = pltpu.make_async_remote_copy(
                src_ref=down_out.at[k, :, span],
                dst_ref=down_in.at[k, :, span],
                send_sem=down_send.at[k, i],
                recv_sem=down_recv.at[k, i],
                device_id={"replica": to},
                device_id_type=MESH,
            )
            down_copies[k, i].start()

    @pl.when(owner_core == core)
    def _():
        up_copy.start()

    tokens_copy.start()
    for copy in weight_copies:
        copy.start()

    for j in range(blocks):
        for table, (cut, size) in zip(tables, cuts):
            down_in[0, j, pl.ds(cut, size)] = table[ids_ref[j]]

    for k, to, _ in peers:
        up_copies[k] = pltpu.make_async_remote_copy(
            src_ref=up_out.at[k],
            dst_ref=up_in.at[lax.rem(me, owners)],
            send_sem=up_send.at[k],
            recv_sem=up_recv.at[lax.rem(me, owners)],
            device_id={"replica": to},
            device_id_type=MESH,
        )

    @pl.when(owner_core == core)
    def _():
        up_copy.wait()
        for k, _, _ in peers:
            for j in range(blocks):
                up_out[k, j] = up_table[all_ids[replicas - k, j]]
            up_copies[k].start()
        for j in range(blocks):
            up_in[lax.rem(me, owners), j] = up_table[ids_ref[j]]

    tokens_copy.wait()
    for copy in weight_copies:
        copy.wait()
    tile = 256

    def base_tile(column):
        return jnp.dot(
            tokens[...],
            weight[:, pl.ds(pl.multiple_of(column, tile), tile)],
            preferred_element_type=jnp.float32,
        )

    @pl.loop(0, half // tile)
    def _(i):
        base_out[:, pl.ds(pl.multiple_of(i * tile, tile), tile)] = base_tile(sibling * half + i * tile)

    base_copy = pltpu.make_async_remote_copy(
        src_ref=base_out,
        dst_ref=base_in,
        send_sem=pair_send.at[0],
        recv_sem=pair_recv.at[0],
        device_id={"tensor": sibling},
        device_id_type=MESH,
    )
    base_copy.start()

    @pl.loop(0, half // tile)
    def _(i):
        base[:, pl.ds(pl.multiple_of(i * tile, tile), tile)] = base_tile(core * half + i * tile)

    def add_part(k, source, first, finish=lambda j: None):
        column = pl.multiple_of(source * part, LANES)
        for j in range(blocks):
            span = pl.ds(j * BLOCK, BLOCK)
            term = lax.dot_general(
                tokens[span, pl.ds(column, part)],
                down_in[k, j],
                (((1,), (1,)), ((), ())),
                preferred_element_type=jnp.float32,
            )
            shrink_out[span, :] = term if first else shrink_out[span, :] + term
            finish(j)

    add_part(0, me, True)
    base_copy.wait()
    base[...] += base_in[...]
    shrink_copies = [
        pltpu.make_async_remote_copy(
            src_ref=shrink_out.at[pl.ds(j * BLOCK, BLOCK)],
            dst_ref=shrink_in.at[pl.ds(j * BLOCK, BLOCK)],
            send_sem=pair_send.at[1 + j],
            recv_sem=pair_recv.at[1 + j],
            device_id={"tensor": sibling},
            device_id_type=MESH,
        )
        for j in range(blocks)
    ]
    for k, _, source in peers[:0:-1]:
        for i in range(len(cuts)):
            down_copies[k, i].wait_recv()
        add_part(k, source, False)
    k, _, source = peers[0]
    for i in range(len(cuts)):
        down_copies[k, i].wait_recv()
    add_part(k, source, False, lambda j: shrink_copies[j].start())

    for s in range(owners):
        arriving = pltpu.make_async_remote_copy(
            src_ref=up_out.at[0],
            dst_ref=up_in.at[s],
            send_sem=up_send.at[0],
            recv_sem=up_recv.at[s],
            device_id={"replica": lax.rem(me + 1, replicas)},
            device_id_type=MESH,
        )

        @pl.when(core * owners + s != me)
        def _():
            arriving.wait_recv()

    for j in range(blocks):
        span = pl.ds(j * BLOCK, BLOCK)
        shrink_copies[j].wait()
        shrunk = (shrink_out[span, :] + shrink_in[span, :]).astype(jnp.bfloat16)
        for s in range(owners):
            delta = jnp.dot(shrunk, up_in[s, j], preferred_element_type=jnp.float32)
            wide = pl.ds(s * columns, columns)
            position = lax.broadcasted_iota(jnp.int32, delta.shape, 0)
            value = jnp.where(position < live_ref[j], base[span, wide] + delta, 0.0)
            out_ref[span, wide] = value.astype(out_ref.dtype)

    for copy in down_copies.values():
        copy.wait_send()

    @pl.when(owner_core == core)
    def _():
        for copy in up_copies.values():
            copy.wait_send()


def fused(replicas, tokens, value_weight, adapter_down, adapter_up, adapter_per_block, block_live):
    rows, features = tokens.shape
    adapters, part, rank = adapter_down.shape
    blocks = rows // BLOCK
    out_width = value_weight.shape[1]
    half = out_width // 2
    columns = adapter_up.shape[2]
    owners = half // columns
    dma = pltpu.SemaphoreType.DMA
    return pl.pallas_call(
        functools.partial(fused_kernel, replicas),
        out_shape=jax.ShapeDtypeStruct((rows, half), jnp.bfloat16),
        in_specs=[pl.BlockSpec(memory_space=pltpu.SMEM)] * 2 + [pl.BlockSpec(memory_space=pl.ANY)] * 4,
        out_specs=pl.BlockSpec(memory_space=pltpu.VMEM),
        scratch_shapes=[
            pltpu.SMEM((replicas, blocks), jnp.int32),
            *[pltpu.VMEM((adapters, size * rank // 4, part), jnp.bfloat16) for _, size in CUTS],
            pltpu.VMEM((adapters, rank, columns), jnp.bfloat16),
            pltpu.VMEM((rows, features), jnp.bfloat16),
            pltpu.VMEM((features, out_width), jnp.bfloat16),
            pltpu.VMEM((replicas, blocks, rank, part), jnp.bfloat16),
            pltpu.VMEM((replicas, blocks, rank, columns), jnp.bfloat16),
            pltpu.VMEM((replicas, blocks, rank, part), jnp.bfloat16),
            pltpu.VMEM((owners, blocks, rank, columns), jnp.bfloat16),
            pltpu.VMEM((rows, half), jnp.float32),
            pltpu.VMEM((rows, half), jnp.float32),
            pltpu.VMEM((rows, half), jnp.float32),
            pltpu.VMEM((rows, rank), jnp.float32),
            pltpu.VMEM((rows, rank), jnp.float32),
            dma((len(CUTS),)),
            dma((4,)),
            dma((replicas,)),
            dma((replicas,)),
            dma((replicas, len(CUTS))),
            dma((replicas, len(CUTS))),
            dma((replicas,)),
            dma((owners,)),
            dma((1 + blocks,)),
            dma((1 + blocks,)),
        ],
        compiler_params=pltpu.CompilerParams(
            collective_id=0, has_side_effects=True, vmem_limit_bytes=56 * 1024 * 1024
        ),
        cost_estimate=pl.CostEstimate(
            flops=2 * rows * features * (out_width + rank), bytes_accessed=32 * 1024 * 1024, transcendentals=0
        ),
    )(adapter_per_block, block_live, tokens, value_weight, jnp.swapaxes(adapter_down, 1, 2), adapter_up)


def spread(replicas, tokens, value_weight, adapter_down, adapter_up, adapter_per_block, block_live):
    cores = lax.axis_size("tensor")
    core = lax.axis_index("tensor")
    rows = tokens.shape[0]
    blocks = rows // BLOCK
    part, rank = adapter_down.shape[1:]
    half = value_weight.shape[1] // cores
    every_id = lax.all_gather(adapter_per_block, "replica", axis=0, tiled=True)
    down = jnp.swapaxes(adapter_down, 1, 2)[every_id]
    down = down.reshape(replicas, blocks, rank, part)
    down = lax.all_to_all(down, "replica", split_axis=0, concat_axis=0, tiled=True)
    up = adapter_up[every_id].reshape(replicas, blocks, rank, -1)
    up = lax.all_to_all(up, "replica", split_axis=0, concat_axis=0, tiled=True)
    owners = replicas // cores
    up = lax.dynamic_slice_in_dim(up, core * owners, owners, 0)
    base = jnp.dot(tokens, value_weight, preferred_element_type=jnp.float32)
    base = lax.psum_scatter(base, "tensor", scatter_dimension=1, tiled=True)
    blocked = tokens.reshape(blocks, BLOCK, replicas, part)
    shrink = jnp.einsum("bksf,sbrf->bkr", blocked, down, preferred_element_type=jnp.float32)
    shrunk = lax.psum(shrink, "tensor").astype(jnp.bfloat16)
    delta = jnp.einsum("bkr,sbrc->bksc", shrunk, up, preferred_element_type=jnp.float32)
    combined = base + delta.reshape(rows, half)
    position = jnp.arange(BLOCK, dtype=jnp.int32)
    live = (position[None, :] < block_live[:, None]).reshape(rows, 1)
    return jnp.where(live, combined, 0.0).astype(jnp.bfloat16)


def local(tokens, value_weight, adapter_down, adapter_up, adapter_per_block, block_live):
    replicas = lax.axis_size("replica")
    cores = lax.axis_size("tensor")
    half = value_weight.shape[1] // cores
    part, columns = adapter_down.shape[1], adapter_up.shape[2]
    aligned = part % LANES == 0 and columns % LANES == 0 and half % 256 == 0
    aligned = aligned and replicas >= 4 and adapter_down.shape[2] % 64 == 0
    inner = fused if aligned and cores == 2 and half % columns == 0 else spread
    return inner(replicas, tokens, value_weight, adapter_down, adapter_up, adapter_per_block, block_live)


def solution(mesh):
    return jax.shard_map(
        local,
        mesh=mesh,
        in_specs=(
            P(("groups", "replica"), "tensor"),
            P("tensor", None),
            P(None, ("tensor", "replica"), None),
            P(None, None, "replica"),
            P(("groups", "replica")),
            P(("groups", "replica")),
        ),
        out_specs=P(("groups", "replica"), "tensor"),
        check_vma=False,
    )
```
